32 devices in a mesh: view: 4 (over z), seg: 8 (over y, x, core).
Axes of the slice: x: 2, y: 2, z: 4, core: 2. Of those that a mesh axis runs over, the one named last changes fastest.
Arguments:
- features: bfloat16 [32, 1369, 1024], P(('view', 'seg')), may hold values from -6 to 6
- block_ids: int32 [32, 8, 2], P(('view', 'seg')), may hold values from 0 to 32, as said below
- patch_rows: int32 [32, 8, 2, 32], P(('view', 'seg')), may hold values from 0 to 1368
- lift_weights: bfloat16 [32, 8, 2, 64, 32], P(('view', 'seg')), may hold values from 0 to 0.5
- coords: int32 [4, 8, 3, 512], P('view', 'seg'), may hold values from 0 to 127, as said below
- w_in: float32 [1024, 768], replicated, may hold values from -0.1875 to 0.1875
- w_query: bfloat16 [768, 768], replicated, may hold values from -1 to 1
- w_key: bfloat16 [768, 768], replicated, may hold values from -1 to 1
- w_value: bfloat16 [768, 768], replicated, may hold values from -0.21875 to 0.21875
- w_out: bfloat16 [768, 768], replicated, may hold values from -0.21875 to 0.21875
- w_up: bfloat16 [768, 3072], replicated, may hold values from -0.21875 to 0.21875
- w_down: bfloat16 [3072, 768], replicated, may hold values from -0.109375 to 0.109375
Outputs:
- encoded: bfloat16 [4, 8, 512, 768], P('view', 'seg')
The draws below stay inside these ranges and needn't reach their ends.
Inputs may be any that keep to these rules, and one draw needn't show every extreme that they name: In each row block_ids[j, s] the live entries (below 32) come first, are distinct and number 1 to 2; the others equal 32. All rows of one destination segment are full. The value 4 * 8 - 1 never occurs. `coords`: the three coordinates of distinct voxels of a 128-cube; their Morton codes rise strictly with the voxel index.
All inputs are finite; a program needn't handle non-finite values.
Results may differ from the reference program's by a relative error of at most 0.007.
Values may be sent and summed in bfloat16 or wider, within the bound.
A program may use at most 128 MiB of HBM per device.

```python
import math
import jax
import jax.numpy as jnp
from jax import lax

C = 1024
D = 768
HEADS = 12
HEAD_DIM = 64
FF = 3072
PATCHES = 1369
BLOCK_PATCHES = 32
BLOCK = 64
CAP = 2
ROWS_DEV = 512
VIEWS = 32
N_VIEW = 4
N_SEG = 8


def draw_block_ids(key, part):
    segment_blocks = N_VIEW * (ROWS_DEV // BLOCK)
    base_key = jax.random.fold_in(key, 11)
    key_scores, key_live, key_full = jax.random.split(base_key, 3)
    scores = jax.random.randint(key_scores, (VIEWS, N_SEG, segment_blocks - 1), 0, 1 << 20)
    scores = scores * (segment_blocks - 1) + jnp.arange(segment_blocks - 1, dtype=jnp.int32)
    order = jnp.argsort(scores, axis=-1)[..., :CAP].astype(jnp.int32)
    live = jax.random.randint(key_live, (VIEWS, N_SEG, 1), 1, CAP + 1)
    full_segment = jax.random.randint(key_full, (), 0, N_SEG)
    live = jnp.where(jnp.arange(N_SEG, dtype=jnp.int32)[None, :, None] == full_segment, CAP, live)
    slot_index = jnp.arange(CAP, dtype=jnp.int32)
    return jnp.where(slot_index < live, order, segment_blocks).astype(jnp.int32)


def draw_coords(key, part):
    voxel_count = N_VIEW * N_SEG * ROWS_DEV
    steps_between = jax.random.randint(jax.random.fold_in(key, 23), (voxel_count,), 1, 8)
    codes = jnp.cumsum(steps_between) - steps_between[0]
    codes = codes.at[-1].set(2097151)
    axes_out = []
    for axis_pos in range(3):
        coordinate = jnp.zeros_like(codes)
        for bit_pos in range(7):
            coordinate = coordinate + codes // (1 << 3 * bit_pos + axis_pos) % 2 * (1 << bit_pos)
        axes_out.append(coordinate)
    stacked = jnp.stack(axes_out, axis=0).reshape(3, N_VIEW, N_SEG, ROWS_DEV)
    return jnp.transpose(stacked, (1, 2, 0, 3)).astype(jnp.int32)


def attention_pair(key):
    base_key = jax.random.fold_in(key, 31)
    key_query = jax.random.fold_in(base_key, 2)
    key_extra = jax.random.fold_in(base_key, 3)
    spread = 1.0 / math.sqrt(D)
    query_part = jax.random.normal(key_query, (D, D), jnp.float32) * spread
    key_part = jax.random.normal(key_extra, (D, D), jnp.float32) * spread
    return (jnp.clip(query_part, -1.0, 1.0), jnp.clip(key_part, -1.0, 1.0))


def draw_w_query(key, part):
    return attention_pair(key)[0].astype(jnp.bfloat16)


def draw_w_key(key, part):
    return attention_pair(key)[1].astype(jnp.bfloat16)


def plant(result, rng, smallest, high):
    longest = result.shape.index(max(result.shape))
    spots = []
    for shift in (0, 1):
        where = [jax.random.randint(jax.random.fold_in(rng, axis), (), 0, length) for axis, length in enumerate(result.shape)]
        where[longest] = (where[longest] + shift) % result.shape[longest]
        spots.append(tuple(where))
    return result.at[spots[0]].set(smallest).at[spots[1]].set(high)


def levels(own_key, dims, cuts, least, high):
    level, own = 1.0, jax.random.fold_in(own_key, 6)
    for dim, parts in cuts:
        steps = jnp.exp(jax.random.uniform(jax.random.fold_in(own, dim), (parts,), jnp.float32, least / len(cuts), high / len(cuts)))
        level = level * jnp.repeat(steps, dims[dim] // parts).reshape([-1 if axis == dim else 1 for axis in range(len(dims))])
    return level


def scatter_about(rng, extent, scale, bound, cuts=(), kind=jnp.bfloat16):
    gain = levels(rng, extent, cuts, -0.22, 0.18) if cuts else 1.0
    entries = jax.random.normal(rng, extent, jnp.float32) * scale * gain
    return jnp.minimum(jnp.maximum(entries, -bound), bound).astype(kind)


def setup_inputs(seed: int = 0) -> dict:
    splits = jax.random.split(jax.random.key(seed), 13)
    return {
        "features": scatter_about(splits[0], (VIEWS, PATCHES, C), 1.0, 6.0, ((0, 32),)),
        "block_ids": draw_block_ids(jax.random.fold_in(splits[12], 71), 0),
        "patch_rows": plant(jax.random.randint(splits[2], (VIEWS, N_SEG, CAP, BLOCK_PATCHES), 0, PATCHES), jax.random.fold_in(splits[2], 1), 0, PATCHES - 1).astype(jnp.int32),
        "lift_weights": jnp.clip(0.5 * jax.random.uniform(splits[3], (VIEWS, N_SEG, CAP, BLOCK, BLOCK_PATCHES), jnp.float32) ** levels(splits[3], (VIEWS, N_SEG, CAP, BLOCK, BLOCK_PATCHES), ((0, 32),), -0.2, 0.2), 0.0, 0.5).astype(jnp.bfloat16),
        "coords": draw_coords(jax.random.fold_in(splits[12], 71), 0),
        "w_in": scatter_about(splits[5], (C, D), C ** -0.5, 0.1875, (), jnp.float32),
        "w_query": draw_w_query(jax.random.fold_in(splits[12], 71), 0),
        "w_key": draw_w_key(jax.random.fold_in(splits[12], 71), 0),
        "w_value": scatter_about(splits[8], (D, D), D ** -0.5, 0.21875),
        "w_out": scatter_about(splits[9], (D, D), D ** -0.5, 0.21875),
        "w_up": scatter_about(splits[10], (D, FF), D ** -0.5, 0.21875),
        "w_down": scatter_about(splits[11], (FF, D), FF ** -0.5, 0.109375),
    }


def normalize(values):
    average = lax.optimization_barrier(jnp.mean(values, axis=-1, keepdims=True))
    centred = values - average
    spread = lax.optimization_barrier(jnp.mean(centred * centred, axis=-1, keepdims=True))
    return (centred * lax.rsqrt(spread + 1e-05)).astype(jnp.bfloat16)

def position_code(places, model_width):
    freq_count = model_width // 6
    frequency = jnp.exp(-math.log(10000.0) * jnp.arange(freq_count, dtype=jnp.float32) / freq_count)
    angles = places.astype(jnp.float32)[:, :, None] * frequency
    pieces = jnp.concatenate([jnp.sin(angles), jnp.cos(angles)], axis=-1)
    return jnp.transpose(pieces, (1, 0, 2)).reshape(places.shape[1], model_width)

def reference(features, block_ids, patch_rows, lift_weights, coords, w_in, w_query, w_key, w_value, w_out, w_up, w_down):
    quarter_blocks = ROWS_DEV // BLOCK
    segment_blocks = N_VIEW * quarter_blocks
    channel_count = features.shape[-1]
    voxel_count = N_VIEW * N_SEG * ROWS_DEV
    segment_index = jnp.arange(N_SEG, dtype=jnp.int32)[:, None]

    def add_view(carry, inputs):
        sums, tallies = carry
        view_table, view_ids, view_rows, view_weights = inputs
        patches = view_table[view_rows].astype(jnp.float32)
        lifted = jnp.einsum('sabk,sakc->sabc', view_weights.astype(jnp.float32), patches).astype(jnp.bfloat16)
        lifted = lax.optimization_barrier(lifted).astype(jnp.float32)
        sums = sums.at[segment_index, view_ids].add(lifted)
        tallies = tallies.at[segment_index, view_ids].add(jnp.ones(view_ids.shape, jnp.float32))
        return ((sums, tallies), None)
    start = (jnp.zeros((N_SEG, segment_blocks + 1, BLOCK, channel_count), jnp.float32), jnp.zeros((N_SEG, segment_blocks + 1), jnp.float32))
    (sums, tallies), _ = lax.scan(add_view, start, (features, block_ids, patch_rows, lift_weights))
    sums = sums[:, :segment_blocks].reshape(N_SEG, N_VIEW, quarter_blocks * BLOCK, channel_count)
    sums = jnp.transpose(sums, (1, 0, 2, 3)).reshape(voxel_count, channel_count)
    tallies = tallies[:, :segment_blocks].reshape(N_SEG, N_VIEW, quarter_blocks)
    tallies = jnp.transpose(tallies, (1, 0, 2)).reshape(-1)
    projected = jnp.dot(sums, w_in, precision=lax.Precision.HIGHEST, preferred_element_type=jnp.float32)
    model_width = projected.shape[1]
    averaged = (projected.reshape(-1, BLOCK, model_width) / jnp.maximum(tallies, 1.0)[:, None, None]).reshape(voxel_count, model_width)
    places = jnp.transpose(coords, (2, 0, 1, 3)).reshape(3, voxel_count)
    stream = averaged + position_code(places, model_width)
    normed = normalize(stream)
    query = jnp.dot(normed, w_query, preferred_element_type=jnp.float32).astype(jnp.bfloat16)
    keys = jnp.dot(normed, w_key, preferred_element_type=jnp.float32).astype(jnp.bfloat16)
    values = jnp.dot(normed, w_value, preferred_element_type=jnp.float32).astype(jnp.bfloat16)
    half = BLOCK // 2

    def windowed(array):
        rolled = jnp.roll(array, -half, axis=0)
        return rolled.reshape(voxel_count // BLOCK, BLOCK, HEADS, HEAD_DIM).astype(jnp.float32)
    scores = jnp.einsum('wqhd,wkhd->whqk', windowed(query), windowed(keys)) / math.sqrt(HEAD_DIM)
    probs = jax.nn.softmax(scores, axis=-1).astype(jnp.bfloat16)
    probs = lax.optimization_barrier(probs).astype(jnp.float32)
    mixed = jnp.einsum('whqk,wkhd->wqhd', probs, windowed(values)).astype(jnp.bfloat16)
    mixed = jnp.roll(mixed.reshape(voxel_count, model_width), half, axis=0)
    attended = stream + jnp.dot(mixed, w_out, preferred_element_type=jnp.float32)
    normed_two = normalize(attended)
    hidden = jax.nn.gelu(jnp.dot(normed_two, w_up, preferred_element_type=jnp.float32), approximate=True).astype(jnp.bfloat16)
    encoded = attended + jnp.dot(hidden, w_down, preferred_element_type=jnp.float32)
    return encoded.astype(jnp.bfloat16).reshape(N_VIEW, N_SEG, ROWS_DEV, model_width)
```

```python
import functools
import math

import jax
import jax.numpy as jnp
from jax import lax
from jax.experimental import pallas as pl
from jax.experimental.pallas import tpu as pltpu
from jax.sharding import PartitionSpec as P

HEAD_DIM = 64
MESH = pl.DeviceIdType.MESH
F32 = jnp.float32
BF16 = jnp.bfloat16
CW = 128
ID_ROWS = 16
VMEM_LIMIT = 56 * 1024 * 1024


def normalize(values):
    average = jnp.mean(values, axis=-1, keepdims=True)
    centred = values - average
    spread = jnp.mean(centred * centred, axis=-1, keepdims=True)
    return (centred * lax.rsqrt(spread + 1e-05)).astype(BF16)


def lift_kernel(
    V, G, cfg,
    feat, idx, w_in, wmsg, places, freq,
    stream_out, ext_out,
    gathered, sb, pp, wm, am, sums_out, sums_in, tal_out, tal_in, acc, halo,
    asend, arecv, zsend, zrecv, ssend, srecv, hsend, hrecv,
):
    KS, BLK, QB, CC = cfg
    rows = QB * BLK
    half = BLK // 2
    me_v = lax.axis_index("view")
    me_g = lax.axis_index("seg")
    outer = (me_v == 0) | (me_v == V - 1)
    middle = jnp.logical_not(outer)
    inner_of = jnp.where(me_v == 0, 1, V - 2)
    outer_of = jnp.where(me_v == 1, 0, V - 1)
    other = V - 1 - me_v
    far = V - 1 - outer_of
    flat = me_v * G + me_g
    nxt = lax.rem(flat + 1, V * G)
    prv = lax.rem(flat + V * G - 1, V * G)
    nxt_id = (nxt // G, lax.rem(nxt, G))
    prv_id = (prv // G, lax.rem(prv, G))

    barrier = pltpu.get_barrier_semaphore()

    def greet(dev):
        pl.semaphore_signal(barrier, inc=1, device_id=dev, device_id_type=MESH)

    for off in range(1, G):
        greet((me_v, lax.rem(me_g + off, G)))
    greet(nxt_id)
    greet(prv_id)

    @pl.when(outer)
    def _():
        greet((inner_of, me_g))

    @pl.when(middle)
    def _():
        greet((outer_of, me_g))
        greet((other, me_g))

    pl.semaphore_wait(barrier, G + 1 + jnp.where(outer, 1, 2))

    def remote(src, dst, s, r, dev):
        return pltpu.make_async_remote_copy(
            src_ref=src, dst_ref=dst, send_sem=s, recv_sem=r,
            device_id=dev, device_id_type=MESH,
        )

    def seg_copy(cc, off):
        peer = lax.rem(me_g + off, G)
        if cc == CC:
            src, dst = wmsg.at[peer], wm.at[me_v, me_g]
        else:
            src, dst = sb.at[cc, peer], pp.at[me_v, cc, me_g]
        return remote(src, dst, asend.at[cc, off], arecv.at[cc, off], (me_v, peer))

    def seg_wait_recv(cc, off):
        src_g = lax.rem(me_g + G - off, G)
        buf = wm.at[me_v, src_g] if cc == CC else pp.at[me_v, cc, src_g]
        remote(buf, buf, asend.at[cc, off], arecv.at[cc, off], (me_v, src_g)).wait_recv()

    def view_copy(z, cc, kind, dev_v):
        buf = wm.at[z] if cc == CC else pp.at[z, cc]
        return remote(buf, buf, zsend.at[kind, cc], zrecv.at[kind, cc], (dev_v, me_g))

    def sum_copy(cc):
        if cc == CC:
            return remote(tal_out, tal_in, ssend.at[cc], srecv.at[cc], (outer_of, me_g))
        return remote(sums_out.at[cc], sums_in.at[cc], ssend.at[cc], srecv.at[cc], (outer_of, me_g))

    for off in range(1, G):
        seg_copy(CC, off).start()
    wm[me_v, me_g] = wmsg[me_g]

    patches = feat.shape[0]
    step = 128
    def gather_step(i, carry):
        at = pl.ds(pl.multiple_of(i * step, step), step)
        picks = idx[at, :]
        hot = (lax.broadcasted_iota(jnp.int32, (step, patches), 1) == picks).astype(F32).astype(BF16)
        gathered[at, :] = jnp.dot(hot, feat[...], preferred_element_type=F32).astype(BF16)
        return carry
    lax.fori_loop(0, G * KS // step, gather_step, 0)

    for cc in range(CC):
        full = w_in[:, cc * CW:(cc + 1) * CW]
        high = full.astype(BF16)
        low = (full - high.astype(F32)).astype(BF16)
        rows_all = gathered[...]
        part = jnp.dot(rows_all, high, preferred_element_type=F32)
        part = part + jnp.dot(rows_all, low, preferred_element_type=F32)
        sb[cc] = part.astype(BF16).reshape(G, KS, CW)
        for off in range(1, G):
            seg_copy(cc, off).start()
        pp[me_v, cc, me_g] = sb[cc, me_g]

    order = [CC] + list(range(CC))
    for cc in order:
        for off in range(1, G):
            seg_wait_recv(cc, off)

        @pl.when(outer)
        def _():
            view_copy(me_v, cc, 0, inner_of).start()

        @pl.when(middle)
        def _():
            view_copy(me_v, cc, 1, other).start()

    lane_low = lax.broadcasted_iota(jnp.int32, (1, 2 * KS), 1) < KS

    def build(slot, z, quarter):
        tally = jnp.zeros((QB, 1), F32)
        for pair in range(G // 2):
            first = wm[z, 2 * pair].astype(F32)
            second = wm[z, 2 * pair + 1].astype(F32)
            a, b = first[:half], second[:half]
            top = jnp.concatenate([a[:, :KS], b[:, :KS]], axis=1)
            bottom = jnp.concatenate([a[:, KS:], b[:, KS:]], axis=1)
            weights = jnp.concatenate([top, bottom], axis=0)
            ids = jnp.where(lane_low, first[half:half + 1], second[half:half + 1])
            base = (quarter * QB).astype(F32)
            cols = slice(pair * 2 * KS, (pair + 1) * 2 * KS)
            for blk in range(QB):
                am[slot, z, blk * BLK:(blk + 1) * BLK, cols] = jnp.where(
                    ids == base + blk, weights, 0.0
                ).astype(BF16)
            blocks = lax.broadcasted_iota(jnp.int32, (QB, 2 * KS), 0).astype(F32) + base
            hits = jnp.where(ids == blocks, 1.0, 0.0)
            tally = tally + jnp.sum(hits, axis=1, keepdims=True)
        return tally * (1.0 / cfg_bp)

    cfg_bp = KS // 2

    def product(slot, z, cc):
        return jnp.dot(am[slot, z], pp[z, cc].reshape(G * KS, CW), preferred_element_type=F32)

    def position(cc):
        angles = places[:, cc // 2:cc // 2 + 1] * freq[...]
        return jnp.sin(angles) if cc % 2 == 0 else jnp.cos(angles)

    def finish(cc, total, tally):
        pos = stream_out[:, cc * CW:(cc + 1) * CW]
        parts = []
        for blk in range(QB):
            count = jnp.maximum(tally[blk:blk + 1, :], 1.0)
            parts.append(total[blk * BLK:(blk + 1) * BLK] / count)
        stream_out[:, cc * CW:(cc + 1) * CW] = jnp.concatenate(parts, axis=0) + pos

    for cc in range(CC):
        stream_out[:, cc * CW:(cc + 1) * CW] = position(cc)

    @pl.when(outer)
    def _():
        own_tally = build(0, me_v, me_v)
        for cc in range(CC):
            acc[:, cc * CW:(cc + 1) * CW] = product(0, me_v, cc)
        remote(tal_in, tal_in, ssend.at[CC], srecv.at[CC], (inner_of, me_g)).wait_recv()
        tally = own_tally + tal_in[:QB, 0:1].astype(F32)
        for cc in range(CC):
            remote(sums_in.at[cc], sums_in.at[cc], ssend.at[cc], srecv.at[cc], (inner_of, me_g)).wait_recv()
            finish(cc, acc[:, cc * CW:(cc + 1) * CW] + sums_in[cc].astype(F32), tally)
        for cc in order:
            view_copy(me_v, cc, 0, inner_of).wait_send()

    @pl.when(middle)
    def _():
        def pass_on(cc):
            view_copy(outer_of, cc, 0, other).wait_recv()
            view_copy(outer_of, cc, 2, other).start()

        pass_on(CC)
        pass_on(0)
        tally = build(0, me_v, me_v) + build(0, outer_of, me_v)
        for_end = build(1, me_v, outer_of)
        pass_on(1)
        view_copy(other, CC, 1, other).wait_recv()
        view_copy(far, CC, 2, other).wait_recv()
        tally = tally + build(0, other, me_v) + build(0, far, me_v)
        for_end = for_end + build(1, other, outer_of) + build(1, far, outer_of)
        tal_out[...] = jnp.concatenate(
            [jnp.broadcast_to(for_end, (QB, 128)), jnp.zeros((ID_ROWS - QB, 128), F32)], axis=0
        ).astype(BF16)
        sum_copy(CC).start()
        for cc in range(2, CC):
            pass_on(cc)
        for cc in range(CC):
            view_copy(other, cc, 1, other).wait_recv()
            view_copy(far, cc, 2, other).wait_recv()
            sums_out[cc] = (
                product(1, me_v, cc) + product(1, other, cc) + product(1, far, cc)
            ).astype(BF16)
            sum_copy(cc).start()
            total = (
                product(0, me_v, cc) + product(0, outer_of, cc)
                + product(0, other, cc) + product(0, far, cc)
            )
            finish(cc, total, tally)
        for cc in order:
            view_copy(me_v, cc, 1, other).wait_send()
            view_copy(outer_of, cc, 2, other).wait_send()
            sum_copy(cc).wait_send()

    for blk in range(QB):
        at = slice(blk * BLK, (blk + 1) * BLK)
        ext_out[half + blk * BLK:half + (blk + 1) * BLK, :] = normalize(stream_out[at, :])
    halo[0] = ext_out[half:2 * half, :]
    halo[1] = ext_out[rows:rows + half, :]
    back = remote(halo.at[0], halo.at[2], hsend.at[0], hrecv.at[0], prv_id)
    ahead = remote(halo.at[1], halo.at[3], hsend.at[1], hrecv.at[1], nxt_id)
    back.start()
    ahead.start()
    for cc in order:
        for off in range(1, G):
            seg_copy(cc, off).wait_send()
    back.wait()
    ahead.wait()
    ext_out[:half, :] = halo[3]
    ext_out[half + rows:, :] = halo[2]


def block_kernel(
    cfg,
    ext, stream, w_query, w_key, w_value, w_out, w_up, w_down,
    encoded,
    vq, vk, vv, vo, vup, vdown, query, keys, values, mixed, attended, second, sem,
):
    BLK = cfg
    half = BLK // 2
    rows, width = stream.shape
    total = ext.shape[0]
    loads = [
        pltpu.make_async_copy(src, dst, sem.at[i])
        for i, (src, dst) in enumerate(
            [(w_query, vq), (w_key, vk), (w_value, vv), (w_out, vo), (w_up, vup), (w_down, vdown)]
        )
    ]
    for load in loads:
        load.start()
    for i, (mat, out) in enumerate([(vq, query), (vk, keys), (vv, values)]):
        loads[i].wait()
        out[...] = jnp.dot(ext[...], mat[...], preferred_element_type=F32).astype(BF16)

    pair = 2 * HEAD_DIM
    low = lax.broadcasted_iota(jnp.int32, (1, pair), 1) < HEAD_DIM
    span = 2 * BLK
    groups = [(at, min(span, total - at)) for at in range(0, total, span)]

    def attend(at, size, cols):
        q = query[pl.ds(at, size), cols].astype(F32)
        k = keys[pl.ds(at, size), cols]
        v = values[pl.ds(at, size), cols]
        same = (
            lax.broadcasted_iota(jnp.int32, (size, size), 0) // BLK
            == lax.broadcasted_iota(jnp.int32, (size, size), 1) // BLK
        )
        outs = []
        for side in range(2):
            mine = low if side == 0 else jnp.logical_not(low)
            qs = jnp.where(mine, q, 0.0).astype(BF16)
            scores = lax.dot_general(
                qs, k, (((1,), (1,)), ((), ())), preferred_element_type=F32
            ) * (1.0 / math.sqrt(HEAD_DIM))
            scores = jnp.where(same, scores, -1e30)
            top = jnp.max(scores, axis=-1, keepdims=True)
            e = jnp.exp(scores - top)
            probs = (e / jnp.sum(e, axis=-1, keepdims=True)).astype(BF16)
            outs.append(jnp.dot(probs, v, preferred_element_type=F32))
        mixed[pl.ds(at, size), cols] = jnp.where(low, outs[0], outs[1]).astype(BF16)

    def head_step(h, carry):
        cols = pl.ds(pl.multiple_of(h * pair, pair), pair)
        for at, size in groups:
            attend(at, size, cols)
        return carry

    lax.fori_loop(0, width // pair, head_step, 0)

    loads[3].wait()
    attended[...] = stream[...] + jnp.dot(
        mixed[half:half + rows, :], vo[...], preferred_element_type=F32
    )
    for at in range(0, rows, BLK):
        second[at:at + BLK, :] = normalize(attended[at:at + BLK, :])
    loads[4].wait()
    loads[5].wait()
    step = 512

    def feed(i, carry):
        at = pl.ds(pl.multiple_of(i * step, step), step)
        up = jnp.dot(second[...], vup[:, at], preferred_element_type=F32)
        hidden = jax.nn.gelu(up, approximate=True).astype(BF16)
        attended[...] += jnp.dot(hidden, vdown[at, :], preferred_element_type=F32)
        return carry

    lax.fori_loop(0, w_up.shape[1] // step, feed, 0)
    encoded[...] = attended[...].astype(BF16)


def shards(
    features, block_ids, patch_rows, lift_weights, coords, w_in,
    w_query, w_key, w_value, w_out, w_up, w_down,
):
    V, G = lax.axis_size("view"), lax.axis_size("seg")
    _, _, cap, blk, bp = lift_weights.shape
    rows = coords.shape[-1]
    channels, width = w_in.shape
    KS, QB, CC, half = cap * bp, rows // blk, width // CW, blk // 2
    freqs = width // 6

    weights = jnp.transpose(lift_weights[0], (0, 2, 1, 3)).reshape(G, 2, half, KS)
    weights = jnp.transpose(weights, (0, 2, 1, 3)).reshape(G, half, 2 * KS)
    ids = jnp.repeat(block_ids[0].astype(BF16), bp, axis=1)
    ids = jnp.broadcast_to(jnp.tile(ids, (1, 2))[:, None, :], (G, ID_ROWS, 2 * KS))
    wmsg = jnp.concatenate([weights, ids], axis=1)
    idx = patch_rows[0].reshape(G * KS, 1)
    places = jnp.transpose(coords[0, 0]).astype(F32)
    freq = jnp.exp(-math.log(10000.0) * jnp.arange(freqs, dtype=F32) / freqs)[None, :]

    vmem = pl.BlockSpec(memory_space=pltpu.VMEM)
    dma = pltpu.SemaphoreType.DMA
    stream, ext = pl.pallas_call(
        functools.partial(lift_kernel, V, G, (KS, blk, QB, CC)),
        out_shape=(
            jax.ShapeDtypeStruct((rows, width), F32),
            jax.ShapeDtypeStruct((rows + blk, width), BF16),
        ),
        in_specs=[vmem] * 6,
        out_specs=(vmem, vmem),
        scratch_shapes=[
            pltpu.VMEM((G * KS, channels), BF16),
            pltpu.VMEM((CC, G, KS, CW), BF16),
            pltpu.VMEM((V, CC, G, KS, CW), BF16),
            pltpu.VMEM((V, G, half + ID_ROWS, 2 * KS), BF16),
            pltpu.VMEM((2, V, rows, G * KS), BF16),
            pltpu.VMEM((CC, rows, CW), BF16),
            pltpu.VMEM((CC, rows, CW), BF16),
            pltpu.VMEM((ID_ROWS, 128), BF16),
            pltpu.VMEM((ID_ROWS, 128), BF16),
            pltpu.VMEM((rows, width), F32),
            pltpu.VMEM((4, half, width), BF16),
            dma((CC + 1, G)),
            dma((CC + 1, G)),
            dma((3, CC + 1)),
            dma((3, CC + 1)),
            dma((CC + 1,)),
            dma((CC + 1,)),
            dma((2,)),
            dma((2,)),
        ],
        compiler_params=pltpu.CompilerParams(
            collective_id=0, has_side_effects=True, vmem_limit_bytes=VMEM_LIMIT
        ),
        name="lift",
    )(features[0], idx, w_in, wmsg, places, freq)

    anyspace = pl.BlockSpec(memory_space=pl.ANY)
    ff = w_up.shape[1]
    encoded = pl.pallas_call(
        functools.partial(block_kernel, blk),
        out_shape=jax.ShapeDtypeStruct((rows, width), BF16),
        in_specs=[vmem, vmem] + [anyspace] * 6,
        out_specs=vmem,
        scratch_shapes=[pltpu.VMEM((width, width), BF16)] * 4
        + [pltpu.VMEM((width, ff), BF16), pltpu.VMEM((ff, width), BF16)]
        + [pltpu.VMEM((rows + blk, width), BF16)] * 4
        + [pltpu.VMEM((rows, width), F32), pltpu.VMEM((rows, width), BF16), dma((6,))],
        compiler_params=pltpu.CompilerParams(vmem_limit_bytes=VMEM_LIMIT),
        name="block",
    )(ext, stream, w_query, w_key, w_value, w_out, w_up, w_down)
    return encoded.reshape(1, 1, rows, width)


def solution(mesh):
    in_specs = (
        P(("view", "seg"), None, None),
        P(("view", "seg"), None, None),
        P(("view", "seg"), None, None, None),
        P(("view", "seg"), None, None, None, None),
        P("view", "seg", None, None),
    ) + (P(),) * 7
    out_specs = P("view", "seg", None, None)
    return jax.shard_map(shards, mesh=mesh, in_specs=in_specs, out_specs=out_specs, check_vma=False)
```

```python
import functools
import math

import jax
import jax.numpy as jnp
from jax import lax
from jax.experimental import pallas as pl
from jax.experimental.pallas import tpu as pltpu
from jax.sharding import PartitionSpec as P

HEAD_DIM = 64
MESH = pl.DeviceIdType.MESH
F32 = jnp.float32
BF16 = jnp.bfloat16
CW = 128
ID_ROWS = 16
FF_STEP = 512
VMEM_LIMIT = 56 * 1024 * 1024


def normalize(values):
    average = jnp.mean(values, axis=-1, keepdims=True)
    centred = values - average
    spread = jnp.mean(centred * centred, axis=-1, keepdims=True)
    return (centred * lax.rsqrt(spread + 1e-05)).astype(BF16)


def whole_kernel(
    V, G, cfg,
    features, patch_rows, block_ids, lift_weights, coords, w_in,
    w_query, w_key, w_value, w_out, w_up, w_down,
    encoded,
    wmsg, sb, pp, wm, sums_out, sums_in, tal_out, tal_in, stream, halo, vq, vk, vv, vo, bias,
    asend, arecv, zsend, zrecv, ssend, srecv, hsend, hrecv, lsem,
):
    KS, BP, BLK, QB, CC = cfg
    rows = QB * BLK
    half = BLK // 2
    width = stream.shape[1]
    total = rows + BLK
    me_v = lax.axis_index("view")
    me_g = lax.axis_index("seg")
    outer = (me_v == 0) | (me_v == V - 1)
    middle = jnp.logical_not(outer)
    inner_of = jnp.where(me_v == 0, 1, V - 2)
    outer_of = jnp.where(me_v == 1, 0, V - 1)
    other = V - 1 - me_v
    far = V - 1 - outer_of
    flat = me_v * G + me_g
    nxt = lax.rem(flat + 1, V * G)
    prv = lax.rem(flat + V * G - 1, V * G)
    nxt_id = (nxt // G, lax.rem(nxt, G))
    prv_id = (prv // G, lax.rem(prv, G))

    loads = [
        pltpu.make_async_copy(a, b, lsem.at[i + 2])
        for i, (a, b) in enumerate([(w_query, vq), (w_key, vk), (w_value, vv), (w_out, vo)])
    ]

    barrier = pltpu.get_barrier_semaphore()

    def remote(src, dst, s, r, dev):
        return pltpu.make_async_remote_copy(
            src_ref=src, dst_ref=dst, send_sem=s, recv_sem=r,
            device_id=dev, device_id_type=MESH,
        )

    def seg_copy(cc, off):
        peer = lax.rem(me_g + off, G)
        if cc == CC:
            src, dst = wmsg.at[peer], wm.at[me_v, me_g]
        else:
            src, dst = sb.at[cc, peer], pp.at[me_v, cc, me_g]
        return remote(src, dst, asend.at[cc, off], arecv.at[cc, off], (me_v, peer))

    def seg_wait_recv(cc, off):
        src_g = lax.rem(me_g + G - off, G)
        buf = wm.at[me_v, src_g] if cc == CC else pp.at[me_v, cc, src_g]
        remote(buf, buf, asend.at[cc, off], arecv.at[cc, off], (me_v, src_g)).wait_recv()

    def view_copy(z, cc, kind, dev_v):
        buf = wm.at[z] if cc == CC else pp.at[z, cc]
        return remote(buf, buf, zsend.at[kind, cc], zrecv.at[kind, cc], (dev_v, me_g))

    def sum_copy(cc):
        if cc == CC:
            return remote(tal_out, tal_in, ssend.at[cc], srecv.at[cc], (outer_of, me_g))
        return remote(sums_out.at[cc], sums_in.at[cc], ssend.at[cc], srecv.at[cc], (outer_of, me_g))

    def to_view(cc):
        for off in range(1, G):
            seg_wait_recv(cc, off)

        @pl.when(outer)
        def _():
            view_copy(me_v, cc, 0, inner_of).start()

        @pl.when(middle)
        def _():
            view_copy(me_v, cc, 1, other).start()

    lane = lax.broadcasted_iota(jnp.int32, (1, 2 * KS), 1)

    def send_patches(feat, win, gathered):
        load_feat = pltpu.make_async_copy(features.at[0], feat, lsem.at[0])
        load_win = pltpu.make_async_copy(w_in, win, lsem.at[1])
        load_feat.start()
        load_win.start()
        def greet(dev):
            pl.semaphore_signal(barrier, inc=1, device_id=dev, device_id_type=MESH)

        for off in range(1, G):
            greet((me_v, lax.rem(me_g + off, G)))
        greet(nxt_id)
        greet(prv_id)

        @pl.when(outer)
        def _():
            greet((inner_of, me_g))

        @pl.when(middle)
        def _():
            greet((outer_of, me_g))
            greet((other, me_g))

        slot_of = lax.rem(lane, KS) // BP
        marks = block_ids[0].astype(F32)
        for s in range(G):
            pieces = [lift_weights[0, s, c].astype(F32) for c in range(KS // BP)]
            turned = jnp.transpose(jnp.concatenate(pieces, axis=0))
            folded = jnp.concatenate([turned[:half], turned[half:]], axis=1)
            row = jnp.zeros((1, 2 * KS), F32)
            for c in range(KS // BP):
                row = jnp.where(slot_of == c, marks[c:c + 1, s:s + 1], row)
            wmsg[s] = jnp.concatenate(
                [folded, jnp.broadcast_to(row, (ID_ROWS, 2 * KS))], axis=0
            ).astype(BF16)

        pl.semaphore_wait(barrier, G + 1 + jnp.where(outer, 1, 2))

        for off in range(1, G):
            seg_copy(CC, off).start()
        wm[me_v, me_g] = wmsg[me_g]

        patches = feat.shape[0]
        picks = jnp.concatenate([patch_rows[0, s].astype(F32) for s in range(G)], axis=0)
        picks = jnp.transpose(picks)
        load_feat.wait()
        step = min(256, G * KS)
        for at in range(0, G * KS, step):
            chosen = jnp.concatenate(
                [picks[:, n:n + 1] for n in range(at // BP, (at + step) // BP)], axis=0
            ).astype(jnp.int32)
            hot = (lax.broadcasted_iota(jnp.int32, (step, patches), 1) == chosen).astype(F32).astype(BF16)
            gathered[at:at + step, :] = jnp.dot(hot, feat[...], preferred_element_type=F32).astype(BF16)

        load_win.wait()
        to_view(CC)
        for group in range(CC // 2):
            full = win[:, group * 2 * CW:(group + 1) * 2 * CW]
            high = full.astype(BF16)
            low = (full - high.astype(F32)).astype(BF16)
            rows_all = gathered[...]
            part = jnp.dot(rows_all, high, preferred_element_type=F32)
            part = part + jnp.dot(rows_all, low, preferred_element_type=F32)
            for side in range(2):
                cc = 2 * group + side
                sb[cc] = part[:, side * CW:(side + 1) * CW].astype(BF16).reshape(G, KS, CW)
                for off in range(1, G):
                    seg_copy(cc, off).start()
                pp[me_v, cc, me_g] = sb[cc, me_g]
            if group > 0:
                to_view(2 * group - 2)
                to_view(2 * group - 1)
        to_view(CC - 2)
        to_view(CC - 1)

    channels = w_in.shape[0]
    pl.run_scoped(
        send_patches,
        pltpu.VMEM(features.shape[1:], BF16),
        pltpu.VMEM((channels, width), F32),
        pltpu.VMEM((G * KS, channels), BF16),
    )
    for load in loads:
        load.start()

    order = [CC] + list(range(CC))
    lane_low = lane < KS

    freq_iota = lax.broadcasted_iota(jnp.int32, (1, CW), 1).astype(F32)
    freq = jnp.exp(-math.log(10000.0) * freq_iota / CW)
    spots = [coords[0, a].astype(F32) for a in range(coords.shape[1])]
    spots = jnp.concatenate(spots + [jnp.zeros((8 - len(spots), rows), F32)], axis=0)
    spots = jnp.transpose(spots)
    for cc in range(CC):
        angles = spots[:, cc // 2:cc // 2 + 1] * freq
        stream[:, cc * CW:(cc + 1) * CW] = jnp.sin(angles) if cc % 2 == 0 else jnp.cos(angles)
    span = 2 * BLK
    groups = [(at, min(span, total - at), min(at, total - span)) for at in range(0, total, span)]
    for at, size, kat in groups:
        row_win = (lax.broadcasted_iota(jnp.int32, (size, span), 0) + at) // BLK
        col_win = (lax.broadcasted_iota(jnp.int32, (size, span), 1) + kat) // BLK
        bias[at:at + size, :] = jnp.where(row_win == col_win, 0.0, -1e30)

    def add_up(am):
        def build(slot, z, quarter):
            tally = jnp.zeros((QB, 1), F32)
            base = (quarter * QB).astype(F32)
            blocks = lax.broadcasted_iota(jnp.int32, (QB, 2 * KS), 0).astype(F32) + base
            for pair in range(G // 2):
                first = wm[z, 2 * pair].astype(F32)
                second = wm[z, 2 * pair + 1].astype(F32)
                a, b = first[:half], second[:half]
                top = jnp.concatenate([a[:, :KS], b[:, :KS]], axis=1)
                bottom = jnp.concatenate([a[:, KS:], b[:, KS:]], axis=1)
                weights = jnp.concatenate([top, bottom], axis=0)
                ids = jnp.where(lane_low, first[half:half + 1], second[half:half + 1])
                cols = slice(pair * 2 * KS, (pair + 1) * 2 * KS)
                for blk in range(QB):
                    am[slot, z, blk * BLK:(blk + 1) * BLK, cols] = jnp.where(
                        ids == base + blk, weights, 0.0
                    ).astype(BF16)
                hits = jnp.where(ids == blocks, 1.0, 0.0)
                tally = tally + jnp.sum(hits, axis=1, keepdims=True)
            return tally * (1.0 / BP)

        def product(slot, z, cc):
            return jnp.dot(am[slot, z], pp[z, cc].reshape(G * KS, CW), preferred_element_type=F32)

        def finish(cc, summed, tally):
            cols = slice(cc * CW, (cc + 1) * CW)
            parts = []
            for blk in range(QB):
                count = jnp.maximum(tally[blk:blk + 1, :], 1.0)
                parts.append(summed[blk * BLK:(blk + 1) * BLK] / count)
            stream[:, cols] = jnp.concatenate(parts, axis=0) + stream[:, cols]

        @pl.when(outer)
        def _():
            own_tally = build(0, me_v, me_v)
            remote(tal_in, tal_in, ssend.at[CC], srecv.at[CC], (inner_of, me_g)).wait_recv()
            tally = own_tally + tal_in[:QB, 0:1].astype(F32)
            for cc in range(CC):
                mine = product(0, me_v, cc)
                remote(sums_in.at[cc], sums_in.at[cc], ssend.at[cc], srecv.at[cc], (inner_of, me_g)).wait_recv()
                finish(cc, mine + sums_in[cc].astype(F32), tally)
            for cc in order:
                view_copy(me_v, cc, 0, inner_of).wait_send()

        @pl.when(middle)
        def _():
            def pass_on(cc):
                view_copy(outer_of, cc, 0, other).wait_recv()
                view_copy(outer_of, cc, 2, other).start()

            pass_on(CC)
            pass_on(0)
            tally = build(0, me_v, me_v) + build(0, outer_of, me_v)
            for_end = build(1, me_v, outer_of)
            pass_on(1)
            view_copy(other, CC, 1, other).wait_recv()
            view_copy(far, CC, 2, other).wait_recv()
            tally = tally + build(0, other, me_v) + build(0, far, me_v)
            for_end = for_end + build(1, other, outer_of) + build(1, far, outer_of)
            tal_out[...] = jnp.concatenate(
                [jnp.broadcast_to(for_end, (QB, 128)), jnp.zeros((ID_ROWS - QB, 128), F32)], axis=0
            ).astype(BF16)
            sum_copy(CC).start()
            for cc in range(2, CC):
                pass_on(cc)
            for cc in range(CC):
                view_copy(other, cc, 1, other).wait_recv()
                early = product(1, me_v, cc) + product(1, other, cc)
                view_copy(far, cc, 2, other).wait_recv()
                sums_out[cc] = (early + product(1, far, cc)).astype(BF16)
                sum_copy(cc).start()
                summed = (
                    product(0, me_v, cc) + product(0, outer_of, cc)
                    + product(0, other, cc) + product(0, far, cc)
                )
                finish(cc, summed, tally)
            for cc in order:
                view_copy(me_v, cc, 1, other).wait_send()
                view_copy(outer_of, cc, 2, other).wait_send()
                sum_copy(cc).wait_send()

    pl.run_scoped(add_up, pltpu.VMEM((2, V, rows, G * KS), BF16))

    def transform(vup, vdown, normed, query, keys, values, mixed, hidden):
        halo[0] = normalize(stream[:half, :])
        halo[1] = normalize(stream[rows - half:, :])
        back = remote(halo.at[0], halo.at[2], hsend.at[0], hrecv.at[0], prv_id)
        ahead = remote(halo.at[1], halo.at[3], hsend.at[1], hrecv.at[1], nxt_id)
        back.start()
        ahead.start()
        load_up = pltpu.make_async_copy(w_up, vup, lsem.at[6])
        load_down = pltpu.make_async_copy(w_down, vdown, lsem.at[7])
        load_up.start()
        load_down.start()
        for at in range(0, rows, BLK):
            normed[at:at + BLK, :] = normalize(stream[at:at + BLK, :])
        query[:half, :] = jnp.zeros((half, width), BF16)
        query[half + rows:, :] = jnp.zeros((half, width), BF16)
        for load, mat, out in zip(loads[:3], (vq, vk, vv), (query, keys, values)):
            load.wait()
            out[half:half + rows, :] = jnp.dot(normed[...], mat[...], preferred_element_type=F32).astype(BF16)
        for cc in order:
            for off in range(1, G):
                seg_copy(cc, off).wait_send()
        back.wait()
        ahead.wait()
        edges = jnp.concatenate([halo[3], halo[2]], axis=0)
        for mat, out in zip((vk, vv), (keys, values)):
            edge = jnp.dot(edges, mat[...], preferred_element_type=F32).astype(BF16)
            out[:half, :] = edge[:half]
            out[half + rows:, :] = edge[half:]

        pair = 2 * HEAD_DIM
        low = lax.broadcasted_iota(jnp.int32, (1, pair), 1) < HEAD_DIM
        scale = 1.0 / math.sqrt(HEAD_DIM)
        on_low = jnp.where(low, scale, 0.0).astype(BF16)
        on_high = jnp.where(low, 0.0, scale).astype(BF16)
        ones = jnp.ones((span, pair), BF16)

        def head_step(h, carry):
            cols = pl.ds(pl.multiple_of(h * pair, pair), pair)
            q, k, v = query[:, cols], keys[:, cols], values[:, cols]
            scores = []
            for at, size, kat in groups:
                qs = q[at:at + size]
                both = jnp.concatenate([qs * on_low, qs * on_high], axis=0)
                mask = bias[at:at + size, :]
                scores.append(lax.dot_general(
                    both, k[kat:kat + span], (((1,), (1,)), ((), ())), preferred_element_type=F32,
                ) + jnp.concatenate([mask, mask], axis=0))
            block = jnp.concatenate(scores, axis=0)
            e = jnp.exp(block - jnp.max(block, axis=-1, keepdims=True)).astype(BF16)
            for at, size, kat in groups:
                right = jnp.concatenate([v[kat:kat + span], ones], axis=1)
                out = jnp.dot(e[2 * at:2 * (at + size)], right, preferred_element_type=F32)
                top, bottom = out[:size], out[size:]
                weighted = jnp.where(low, top[:, :pair], bottom[:, :pair])
                sums = jnp.where(low, top[:, pair:], bottom[:, pair:])
                mixed[at:at + size, cols] = (weighted / sums).astype(BF16)
            return carry

        lax.fori_loop(0, width // pair, head_step, 0, unroll=2)

        loads[3].wait()
        stream[...] = stream[...] + jnp.dot(
            mixed[half:half + rows, :], vo[...], preferred_element_type=F32
        )
        for at in range(0, rows, BLK):
            normed[at:at + BLK, :] = normalize(stream[at:at + BLK, :])
        load_up.wait()
        load_down.wait()
        step = hidden.shape[2]
        count = vup.shape[1] // step

        def down(i):
            stream[...] += jnp.dot(
                hidden[i % 2], vdown[i * step:(i + 1) * step, :], preferred_element_type=F32
            )

        for i in range(count):
            up = jnp.dot(normed[...], vup[:, i * step:(i + 1) * step], preferred_element_type=F32)
            if i > 0:
                down(i - 1)
            hidden[i % 2] = jax.nn.gelu(up, approximate=True).astype(BF16)
        encoded[...] = (stream[...] + jnp.dot(
            hidden[(count - 1) % 2], vdown[(count - 1) * step:, :], preferred_element_type=F32
        )).astype(BF16)

    extended = pltpu.VMEM((total, width), BF16)
    pl.run_scoped(
        transform,
        pltpu.VMEM(w_up.shape, BF16),
        pltpu.VMEM(w_down.shape, BF16),
        pltpu.VMEM((rows, width), BF16),
        extended, extended, extended, extended,
        pltpu.VMEM((2, rows, FF_STEP), BF16),
    )


def shards(
    features, block_ids, patch_rows, lift_weights, coords, w_in,
    w_query, w_key, w_value, w_out, w_up, w_down,
):
    V, G = lax.axis_size("view"), lax.axis_size("seg")
    _, _, cap, blk, bp = lift_weights.shape
    rows = coords.shape[-1]
    width = w_in.shape[1]
    KS, QB, CC, half = cap * bp, rows // blk, width // CW, blk // 2
    vmem = pl.BlockSpec(memory_space=pltpu.VMEM)
    anyspace = pl.BlockSpec(memory_space=pl.ANY)
    dma = pltpu.SemaphoreType.DMA
    encoded = pl.pallas_call(
        functools.partial(whole_kernel, V, G, (KS, bp, blk, QB, CC)),
        out_shape=jax.ShapeDtypeStruct((rows, width), BF16),
        in_specs=[anyspace] + [vmem] * 4 + [anyspace] * 7,
        out_specs=vmem,
        scratch_shapes=[
            pltpu.VMEM((G, half + ID_ROWS, 2 * KS), BF16),
            pltpu.VMEM((CC, G, KS, CW), BF16),
            pltpu.VMEM((V, CC, G, KS, CW), BF16),
            pltpu.VMEM((V, G, half + ID_ROWS, 2 * KS), BF16),
            pltpu.VMEM((CC, rows, CW), BF16),
            pltpu.VMEM((CC, rows, CW), BF16),
            pltpu.VMEM((ID_ROWS, 128), BF16),
            pltpu.VMEM((ID_ROWS, 128), BF16),
            pltpu.VMEM((rows, width), F32),
            pltpu.VMEM((4, half, width), BF16),
        ]
        + [pltpu.VMEM((width, width), BF16)] * 4
        + [
            pltpu.VMEM((rows + blk, 2 * blk), F32),
            dma((CC + 1, G)),
            dma((CC + 1, G)),
            dma((3, CC + 1)),
            dma((3, CC + 1)),
            dma((CC + 1,)),
            dma((CC + 1,)),
            dma((2,)),
            dma((2,)),
            dma((8,)),
        ],
        compiler_params=pltpu.CompilerParams(
            collective_id=0, has_side_effects=True, vmem_limit_bytes=VMEM_LIMIT
        ),
        name="voxel_block",
    )(
        features, patch_rows, jnp.transpose(block_ids, (0, 2, 1)),
        jnp.transpose(lift_weights, (0, 1, 2, 4, 3)), jnp.transpose(coords, (0, 2, 1, 3)), w_in,
        w_query, w_key, w_value, w_out, w_up, w_down,
    )
    return encoded.reshape(1, 1, rows, width)


def solution(mesh):
    in_specs = (
        P(("view", "seg"), None, None),
        P(("view", "seg"), None, None),
        P(("view", "seg"), None, None, None),
        P(("view", "seg"), None, None, None, None),
        P("view", "seg", None, None),
    ) + (P(),) * 7
    out_specs = P("view", "seg", None, None)
    return jax.shard_map(shards, mesh=mesh, in_specs=in_specs, out_specs=out_specs, check_vma=False)
```

```python
import functools
import math

import jax
import jax.numpy as jnp
from jax import lax
from jax.experimental import pallas as pl
from jax.experimental.pallas import tpu as pltpu
from jax.sharding import PartitionSpec as P

HEAD_DIM = 64
MESH = pl.DeviceIdType.MESH
F32 = jnp.float32
BF16 = jnp.bfloat16
CW = 128
ID_ROWS = 16
FF_STEP = 768
VMEM_LIMIT = 56 * 1024 * 1024


def normalize(values):
    average = jnp.mean(values, axis=-1, keepdims=True)
    centred = values - average
    spread = jnp.mean(centred * centred, axis=-1, keepdims=True)
    return (centred * lax.rsqrt(spread + 1e-05)).astype(BF16)


def whole_kernel(
    V, G, cfg,
    features, patch_rows, block_ids, lift_weights, coords, w_in,
    w_query, w_key, w_value, w_out, w_up, w_down,
    encoded,
    wmsg, sb, pp, wm, sums_out, sums_in, tal_out, tal_in, stream, halo, vq, vk, vv, vo, bias,
    asend, arecv, zsend, zrecv, ssend, srecv, hsend, hrecv, lsem,
):
    KS, BP, BLK, QB, CC = cfg
    rows = QB * BLK
    half = BLK // 2
    width = stream.shape[1]
    total = rows + BLK
    me_v = lax.axis_index("view")
    me_g = lax.axis_index("seg")
    outer = (me_v == 0) | (me_v == V - 1)
    middle = jnp.logical_not(outer)
    inner_of = jnp.where(me_v == 0, 1, V - 2)
    outer_of = jnp.where(me_v == 1, 0, V - 1)
    other = V - 1 - me_v
    far = V - 1 - outer_of
    flat = me_v * G + me_g
    nxt = lax.rem(flat + 1, V * G)
    prv = lax.rem(flat + V * G - 1, V * G)
    nxt_id = (nxt // G, lax.rem(nxt, G))
    prv_id = (prv // G, lax.rem(prv, G))

    loads = [
        pltpu.make_async_copy(a, b, lsem.at[i + 2])
        for i, (a, b) in enumerate([(w_query, vq), (w_key, vk), (w_value, vv), (w_out, vo)])
    ]

    barrier = pltpu.get_barrier_semaphore()

    def remote(src, dst, s, r, dev):
        return pltpu.make_async_remote_copy(
            src_ref=src, dst_ref=dst, send_sem=s, recv_sem=r,
            device_id=dev, device_id_type=MESH,
        )

    def seg_copy(cc, off):
        peer = lax.rem(me_g + off, G)
        if cc == CC:
            src, dst = wmsg.at[peer], wm.at[me_v, me_g]
        else:
            src, dst = sb.at[cc, peer], pp.at[me_v, cc, me_g]
        return remote(src, dst, asend.at[cc, off], arecv.at[cc, off], (me_v, peer))

    def seg_wait_recv(cc, off):
        src_g = lax.rem(me_g + G - off, G)
        buf = wm.at[me_v, src_g] if cc == CC else pp.at[me_v, cc, src_g]
        remote(buf, buf, asend.at[cc, off], arecv.at[cc, off], (me_v, src_g)).wait_recv()

    def view_copy(z, cc, kind, dev_v):
        buf = wm.at[z] if cc == CC else pp.at[z, cc]
        return remote(buf, buf, zsend.at[kind, cc], zrecv.at[kind, cc], (dev_v, me_g))

    def sum_copy(cc):
        if cc == CC:
            return remote(tal_out, tal_in, ssend.at[cc], srecv.at[cc], (outer_of, me_g))
        return remote(sums_out.at[cc], sums_in.at[cc], ssend.at[cc], srecv.at[cc], (outer_of, me_g))

    def to_view(cc):
        for off in range(1, G):
            seg_wait_recv(cc, off)

        @pl.when(outer)
        def _():
            view_copy(me_v, cc, 0, inner_of).start()

        @pl.when(middle)
        def _():
            view_copy(me_v, cc, 1, other).start()

    lane = lax.broadcasted_iota(jnp.int32, (1, 2 * KS), 1)

    def send_patches(feat, win, gathered):
        load_feat = pltpu.make_async_copy(features.at[0], feat, lsem.at[0])
        load_win = pltpu.make_async_copy(w_in, win, lsem.at[1])
        load_feat.start()
        load_win.start()
        def greet(dev):
            pl.semaphore_signal(barrier, inc=1, device_id=dev, device_id_type=MESH)

        for off in range(1, G):
            greet((me_v, lax.rem(me_g + off, G)))
        greet(nxt_id)
        greet(prv_id)

        @pl.when(outer)
        def _():
            greet((inner_of, me_g))

        @pl.when(middle)
        def _():
            greet((outer_of, me_g))
            greet((other, me_g))

        slot_of = lax.rem(lane, KS) // BP
        marks = block_ids[0].astype(F32)
        for s in range(G):
            pieces = [lift_weights[0, s, c].astype(F32) for c in range(KS // BP)]
            turned = jnp.transpose(jnp.concatenate(pieces, axis=0))
            folded = jnp.concatenate([turned[:half], turned[half:]], axis=1)
            row = jnp.zeros((1, 2 * KS), F32)
            for c in range(KS // BP):
                row = jnp.where(slot_of == c, marks[c:c + 1, s:s + 1], row)
            wmsg[s] = jnp.concatenate(
                [folded, jnp.broadcast_to(row, (ID_ROWS, 2 * KS))], axis=0
            ).astype(BF16)

        pl.semaphore_wait(barrier, G + 1 + jnp.where(outer, 1, 2))

        for off in range(1, G):
            seg_copy(CC, off).start()
        wm[me_v, me_g] = wmsg[me_g]

        patches = feat.shape[0]
        picks = jnp.concatenate([patch_rows[0, s].astype(F32) for s in range(G)], axis=0)
        picks = jnp.transpose(picks)
        load_feat.wait()
        step = min(256, G * KS)
        for at in range(0, G * KS, step):
            chosen = jnp.concatenate(
                [picks[:, n:n + 1] for n in range(at // BP, (at + step) // BP)], axis=0
            ).astype(jnp.int32)
            hot = (lax.broadcasted_iota(jnp.int32, (step, patches), 1) == chosen).astype(F32).astype(BF16)
            gathered[at:at + step, :] = jnp.dot(hot, feat[...], preferred_element_type=F32).astype(BF16)

        load_win.wait()
        to_view(CC)
        for group in range(CC // 2):
            full = win[:, group * 2 * CW:(group + 1) * 2 * CW]
            high = full.astype(BF16)
            low = (full - high.astype(F32)).astype(BF16)
            rows_all = gathered[...]
            part = jnp.dot(rows_all, high, preferred_element_type=F32)
            part = part + jnp.dot(rows_all, low, preferred_element_type=F32)
            for side in range(2):
                cc = 2 * group + side
                sb[cc] = part[:, side * CW:(side + 1) * CW].astype(BF16).reshape(G, KS, CW)
                for off in range(1, G):
                    seg_copy(cc, off).start()
                pp[me_v, cc, me_g] = sb[cc, me_g]
            if group > 0:
                to_view(2 * group - 2)
                to_view(2 * group - 1)
        to_view(CC - 2)
        to_view(CC - 1)

    channels = w_in.shape[0]
    pl.run_scoped(
        send_patches,
        pltpu.VMEM(features.shape[1:], BF16),
        pltpu.VMEM((channels, width), F32),
        pltpu.VMEM((G * KS, channels), BF16),
    )
    for load in loads:
        load.start()

    order = [CC] + list(range(CC))
    lane_low = lane < KS

    freq_iota = lax.broadcasted_iota(jnp.int32, (1, CW), 1).astype(F32)
    freq = jnp.exp(-math.log(10000.0) * freq_iota / CW)
    spots = [coords[0, a].astype(F32) for a in range(coords.shape[1])]
    spots = jnp.concatenate(spots + [jnp.zeros((8 - len(spots), rows), F32)], axis=0)
    spots = jnp.transpose(spots)
    for cc in range(CC):
        angles = spots[:, cc // 2:cc // 2 + 1] * freq
        stream[:, cc * CW:(cc + 1) * CW] = jnp.sin(angles) if cc % 2 == 0 else jnp.cos(angles)
    span = 2 * BLK
    groups = [(at, min(span, total - at), min(at, total - span)) for at in range(0, total, span)]
    for at, size, kat in groups:
        row_win = (lax.broadcasted_iota(jnp.int32, (size, span), 0) + at) // BLK
        col_win = (lax.broadcasted_iota(jnp.int32, (size, span), 1) + kat) // BLK
        bias[at:at + size, :] = jnp.where(row_win == col_win, 0.0, -1e30)

    def add_up(am):
        def build(slot, z, quarter):
            tally = jnp.zeros((QB, 1), F32)
            base = (quarter * QB).astype(F32)
            blocks = lax.broadcasted_iota(jnp.int32, (QB, 2 * KS), 0).astype(F32) + base
            for pair in range(G // 2):
                first = wm[z, 2 * pair].astype(F32)
                second = wm[z, 2 * pair + 1].astype(F32)
                a, b = first[:half], second[:half]
                top = jnp.concatenate([a[:, :KS], b[:, :KS]], axis=1)
                bottom = jnp.concatenate([a[:, KS:], b[:, KS:]], axis=1)
                weights = jnp.concatenate([top, bottom], axis=0)
                ids = jnp.where(lane_low, first[half:half + 1], second[half:half + 1])
                cols = slice(pair * 2 * KS, (pair + 1) * 2 * KS)
                for blk in range(QB):
                    am[slot, z, blk * BLK:(blk + 1) * BLK, cols] = jnp.where(
                        ids == base + blk, weights, 0.0
                    ).astype(BF16)
                hits = jnp.where(ids == blocks, 1.0, 0.0)
                tally = tally + jnp.sum(hits, axis=1, keepdims=True)
            return tally * (1.0 / BP)

        def product(slot, z, cc):
            return jnp.dot(am[slot, z], pp[z, cc].reshape(G * KS, CW), preferred_element_type=F32)

        def finish(cc, summed, tally):
            cols = slice(cc * CW, (cc + 1) * CW)
            parts = []
            for blk in range(QB):
                count = jnp.maximum(tally[blk:blk + 1, :], 1.0)
                parts.append(summed[blk * BLK:(blk + 1) * BLK] / count)
            stream[:, cols] = jnp.concatenate(parts, axis=0) + stream[:, cols]

        @pl.when(outer)
        def _():
            own_tally = build(0, me_v, me_v)
            remote(tal_in, tal_in, ssend.at[CC], srecv.at[CC], (inner_of, me_g)).wait_recv()
            tally = own_tally + tal_in[:QB, 0:1].astype(F32)
            for cc in range(CC):
                mine = product(0, me_v, cc)
                remote(sums_in.at[cc], sums_in.at[cc], ssend.at[cc], srecv.at[cc], (inner_of, me_g)).wait_recv()
                finish(cc, mine + sums_in[cc].astype(F32), tally)
            for cc in order:
                view_copy(me_v, cc, 0, inner_of).wait_send()

        @pl.when(middle)
        def _():
            def pass_on(cc):
                view_copy(outer_of, cc, 0, other).wait_recv()
                view_copy(outer_of, cc, 2, other).start()

            pass_on(CC)
            pass_on(0)
            tally = build(0, me_v, me_v) + build(0, outer_of, me_v)
            for_end = build(1, me_v, outer_of)
            pass_on(1)
            view_copy(other, CC, 1, other).wait_recv()
            view_copy(far, CC, 2, other).wait_recv()
            tally = tally + build(0, other, me_v) + build(0, far, me_v)
            for_end = for_end + build(1, other, outer_of) + build(1, far, outer_of)
            tal_out[...] = jnp.concatenate(
                [jnp.broadcast_to(for_end, (QB, 128)), jnp.zeros((ID_ROWS - QB, 128), F32)], axis=0
            ).astype(BF16)
            sum_copy(CC).start()
            for cc in range(2, CC):
                pass_on(cc)
            for cc in range(CC):
                view_copy(other, cc, 1, other).wait_recv()
                early = product(1, me_v, cc) + product(1, other, cc)
                most = product(0, me_v, cc) + product(0, outer_of, cc) + product(0, other, cc)
                view_copy(far, cc, 2, other).wait_recv()
                sums_out[cc] = (early + product(1, far, cc)).astype(BF16)
                sum_copy(cc).start()
                summed = most + product(0, far, cc)
                finish(cc, summed, tally)
            for cc in order:
                view_copy(me_v, cc, 1, other).wait_send()
                view_copy(outer_of, cc, 2, other).wait_send()
                sum_copy(cc).wait_send()

    pl.run_scoped(add_up, pltpu.VMEM((2, V, rows, G * KS), BF16))

    def transform(vup, vdown, normed, query, keys, values, mixed, hidden):
        halo[0] = normalize(stream[:half, :])
        halo[1] = normalize(stream[rows - half:, :])
        back = remote(halo.at[0], halo.at[2], hsend.at[0], hrecv.at[0], prv_id)
        ahead = remote(halo.at[1], halo.at[3], hsend.at[1], hrecv.at[1], nxt_id)
        back.start()
        ahead.start()
        load_up = pltpu.make_async_copy(w_up, vup, lsem.at[6])
        load_down = pltpu.make_async_copy(w_down, vdown, lsem.at[7])
        load_up.start()
        load_down.start()
        for at in range(0, rows, BLK):
            normed[at:at + BLK, :] = normalize(stream[at:at + BLK, :])
        query[:half, :] = jnp.zeros((half, width), BF16)
        query[half + rows:, :] = jnp.zeros((half, width), BF16)
        for load, mat, out in zip(loads[:3], (vq, vk, vv), (query, keys, values)):
            load.wait()
            out[half:half + rows, :] = jnp.dot(normed[...], mat[...], preferred_element_type=F32).astype(BF16)
        for cc in order:
            for off in range(1, G):
                seg_copy(cc, off).wait_send()
        back.wait()
        ahead.wait()
        edges = jnp.concatenate([halo[3], halo[2]], axis=0)
        for mat, out in zip((vk, vv), (keys, values)):
            edge = jnp.dot(edges, mat[...], preferred_element_type=F32).astype(BF16)
            out[:half, :] = edge[:half]
            out[half + rows:, :] = edge[half:]

        pair = 2 * HEAD_DIM
        low = lax.broadcasted_iota(jnp.int32, (1, pair), 1) < HEAD_DIM
        scale = 1.0 / math.sqrt(HEAD_DIM)
        on_low = jnp.where(low, scale, 0.0).astype(BF16)
        on_high = jnp.where(low, 0.0, scale).astype(BF16)
        ones = jnp.ones((span, pair), BF16)

        def head_step(h, carry):
            cols = pl.ds(pl.multiple_of(h * pair, pair), pair)
            q, k, v = query[:, cols], keys[:, cols], values[:, cols]
            scores = []
            for at, size, kat in groups:
                qs = q[at:at + size]
                both = jnp.concatenate([qs * on_low, qs * on_high], axis=0)
                mask = bias[at:at + size, :]
                scores.append(lax.dot_general(
                    both, k[kat:kat + span], (((1,), (1,)), ((), ())), preferred_element_type=F32,
                ) + jnp.concatenate([mask, mask], axis=0))
            block = jnp.concatenate(scores, axis=0)
            e = jnp.exp(block - jnp.max(block, axis=-1, keepdims=True)).astype(BF16)
            for at, size, kat in groups:
                right = jnp.concatenate([v[kat:kat + span], ones], axis=1)
                out = jnp.dot(e[2 * at:2 * (at + size)], right, preferred_element_type=F32)
                top, bottom = out[:size], out[size:]
                weighted = jnp.where(low, top[:, :pair], bottom[:, :pair])
                sums = jnp.where(low, top[:, pair:], bottom[:, pair:])
                mixed[at:at + size, cols] = (weighted / sums).astype(BF16)
            return carry

        lax.fori_loop(0, width // pair, head_step, 0, unroll=2)

        loads[3].wait()
        stream[...] = stream[...] + jnp.dot(
            mixed[half:half + rows, :], vo[...], preferred_element_type=F32
        )
        for at in range(0, rows, BLK):
            normed[at:at + BLK, :] = normalize(stream[at:at + BLK, :])
        load_up.wait()
        load_down.wait()
        step = hidden.shape[2]
        count = vup.shape[1] // step

        def down(i):
            stream[...] += jnp.dot(
                hidden[i % 2], vdown[i * step:(i + 1) * step, :], preferred_element_type=F32
            )

        for i in range(count):
            up = jnp.dot(normed[...], vup[:, i * step:(i + 1) * step], preferred_element_type=F32)
            if i > 0:
                down(i - 1)
            hidden[i % 2] = jax.nn.gelu(up, approximate=True).astype(BF16)
        encoded[...] = stream[...] + jnp.dot(
            hidden[(count - 1) % 2], vdown[(count - 1) * step:, :], preferred_element_type=F32
        )

    extended = pltpu.VMEM((total, width), BF16)
    pl.run_scoped(
        transform,
        pltpu.VMEM(w_up.shape, BF16),
        pltpu.VMEM(w_down.shape, BF16),
        pltpu.VMEM((rows, width), BF16),
        extended, extended, extended, extended,
        pltpu.VMEM((2, rows, FF_STEP), BF16),
    )


def shards(
    features, block_ids, patch_rows, lift_weights, coords, w_in,
    w_query, w_key, w_value, w_out, w_up, w_down,
):
    V, G = lax.axis_size("view"), lax.axis_size("seg")
    _, _, cap, blk, bp = lift_weights.shape
    rows = coords.shape[-1]
    width = w_in.shape[1]
    KS, QB, CC, half = cap * bp, rows // blk, width // CW, blk // 2
    vmem = pl.BlockSpec(memory_space=pltpu.VMEM)
    anyspace = pl.BlockSpec(memory_space=pl.ANY)
    dma = pltpu.SemaphoreType.DMA
    encoded = pl.pallas_call(
        functools.partial(whole_kernel, V, G, (KS, bp, blk, QB, CC)),
        out_shape=jax.ShapeDtypeStruct((rows, width), F32),
        in_specs=[anyspace] + [vmem] * 4 + [anyspace] * 7,
        out_specs=vmem,
        scratch_shapes=[
            pltpu.VMEM((G, half + ID_ROWS, 2 * KS), BF16),
            pltpu.VMEM((CC, G, KS, CW), BF16),
            pltpu.VMEM((V, CC, G, KS, CW), BF16),
            pltpu.VMEM((V, G, half + ID_ROWS, 2 * KS), BF16),
            pltpu.VMEM((CC, rows, CW), BF16),
            pltpu.VMEM((CC, rows, CW), BF16),
            pltpu.VMEM((ID_ROWS, 128), BF16),
            pltpu.VMEM((ID_ROWS, 128), BF16),
            pltpu.VMEM((rows, width), F32),
            pltpu.VMEM((4, half, width), BF16),
        ]
        + [pltpu.VMEM((width, width), BF16)] * 4
        + [
            pltpu.VMEM((rows + blk, 2 * blk), F32),
            dma((CC + 1, G)),
            dma((CC + 1, G)),
            dma((3, CC + 1)),
            dma((3, CC + 1)),
            dma((CC + 1,)),
            dma((CC + 1,)),
            dma((2,)),
            dma((2,)),
            dma((8,)),
        ],
        compiler_params=pltpu.CompilerParams(
            collective_id=0, has_side_effects=True, vmem_limit_bytes=VMEM_LIMIT
        ),
        name="voxel_block",
    )(
        features, patch_rows, jnp.transpose(block_ids, (0, 2, 1)),
        jnp.transpose(lift_weights, (0, 1, 2, 4, 3)), jnp.transpose(coords, (0, 2, 1, 3)), w_in,
        w_query, w_key, w_value, w_out, w_up, w_down,
    )
    return encoded.astype(BF16).reshape(1, 1, rows, width)


def solution(mesh):
    in_specs = (
        P(("view", "seg"), None, None),
        P(("view", "seg"), None, None),
        P(("view", "seg"), None, None, None),
        P(("view", "seg"), None, None, None, None),
        P("view", "seg", None, None),
    ) + (P(),) * 7
    out_specs = P("view", "seg", None, None)
    return jax.shard_map(shards, mesh=mesh, in_specs=in_specs, out_specs=out_specs, check_vma=False)
```
